32 devices in a mesh: vid: 2 (over x), tm: 16 (over z, y, core).
Axes of the slice: x: 2, y: 2, z: 4, core: 2. Of those that a mesh axis runs over, the one named last changes fastest.
Arguments:
- queries: bfloat16 [4096, 1536], P(('vid', 'tm')), parts along dimension 0, may hold values from -6 to 6
- keys: bfloat16 [4096, 1536], P(('vid', 'tm')), parts along dimension 0, may hold values from -6 to 6
- values: bfloat16 [4096, 1536], P(('vid', 'tm')), parts along dimension 0, may hold values from -6 to 6
- far_picks: int32 [64, 8], P(('vid', 'tm')), parts along dimension 0, may hold values from 0 to 1
- out_weight: bfloat16 [1536, 1536], replicated, may hold values from -0.15625 to 0.15625
Outputs:
- mixed: bfloat16 [4096, 1536], P(('vid', 'tm')), parts along dimension 0
The draws below stay inside these ranges and needn't reach their ends.
There are 2 independent parts, one for each index of `vid`. The reference program is written for one: setup_inputs(seed, part) draws one part's arguments, and reference() takes and returns one part's arrays. A program takes and returns all parts, laid end to end along the dimension named above; an argument that names none is the same for every part. Nothing has to cross between parts.
All inputs are finite; a program needn't handle non-finite values.
Results may differ from the reference program's by a relative error of at most 0.0056.
Values may be sent and summed in bfloat16 or wider, within the bound.
No kernel may reach another device: no remote copies, remote signals or barrier semaphores. Data moves between devices by JAX's collectives and lax.ppermute only.
A program may use at most 64 MiB of HBM per device.

```python
import jax
import jax.numpy as jnp
from jax import lax

D = 1536
HEADS = 12
HEAD_DIM = 128
BLK = 64
LEVELS = 2
PICKS = 2
TOK_DEV = 128
FAR = 8
NB_DEV = 2
TOKENS = 2048
N_TM = 16


def paired_draw(key):
    base_key = jax.random.fold_in(key, 101)
    first_key, second_key = jax.random.split(base_key, 2)
    full_shape = (TOKENS, D)
    query_raw = jnp.clip(jax.random.normal(first_key, full_shape, jnp.float32), -5.0, 5.0)
    key_raw = jnp.clip(jax.random.normal(second_key, full_shape, jnp.float32), -5.0, 5.0)
    return (jnp.clip(query_raw, -6.0, 6.0), jnp.clip(key_raw, -6.0, 6.0))


def draw_queries(key, part):
    return paired_draw(key)[0].astype(jnp.bfloat16)


def draw_keys(key, part):
    return paired_draw(key)[1].astype(jnp.bfloat16)


def place_ends(drawn, own_key, low, high):
    longest = drawn.shape.index(max(drawn.shape))
    spots = []
    for shift in (0, 1):
        where = [jax.random.randint(jax.random.fold_in(own_key, axis), (), 0, length) for axis, length in enumerate(drawn.shape)]
        where[longest] = (where[longest] + shift) % drawn.shape[longest]
        spots.append(tuple(where))
    return drawn.at[spots[0]].set(low).at[spots[1]].set(high)


def levels(key, extent, cuts, smallest, largest):
    level = 1.0
    for axis_at, parts in cuts:
        draws = jax.random.uniform(jax.random.fold_in(jax.random.fold_in(key, 6), axis_at), (parts,), jnp.float32, smallest / len(cuts), largest / len(cuts))
        level = level * jnp.repeat(jnp.exp(draws), extent[axis_at] // parts).reshape((-1,) + (1,) * (len(extent) - 1 - axis_at))
    return level


def centred(key, extent, scale, reach, cuts=(), kind=jnp.bfloat16):
    drawn = scale * jax.random.normal(key, extent, jnp.float32)
    if cuts:
        drawn = drawn * levels(key, extent, cuts, -0.22, 0.18)
    return jnp.clip(drawn, -reach, reach).astype(kind)


def setup_inputs(seed: int = 0, part: int = 0) -> dict:
    key_of = jax.random.split(jax.random.key(seed), 6)
    own_keys = jax.random.split(jax.random.fold_in(key_of[5], part), 6)
    queries = draw_queries(jax.random.fold_in(jax.random.fold_in(key_of[5], part), 71), part)
    keys = draw_keys(jax.random.fold_in(jax.random.fold_in(key_of[5], part), 71), part)
    values = centred(own_keys[2], (TOKENS, D), 1.0, 6.0, ((0, 16),))
    far_picks = place_ends(jax.random.randint(own_keys[3], (TOKENS // BLK, FAR), 0, NB_DEV), jax.random.fold_in(own_keys[3], 1), 0, NB_DEV - 1).astype(jnp.int32)
    out_weight = centred(key_of[4], (D, D), D ** -0.5, 0.15625)
    return {"queries": queries, "keys": keys, "values": values, "far_picks": far_picks, "out_weight": out_weight}


def far_offsets():
    offset_list = []
    for column in range(FAR):
        magnitude = 2 ** (1 + (column // PICKS) % LEVELS)
        offset_list.append(-magnitude if column < FAR // 2 else magnitude)
    return offset_list


def attend(query_rows, near_pair, near_valid, far_pair, far_valid, out_weight):
    blocks = query_rows.shape[0] // BLK
    scale = HEAD_DIM ** -0.5
    query_heads = query_rows.reshape(blocks, BLK, HEADS, HEAD_DIM).astype(jnp.float32)
    near_keys = near_pair[0].reshape(-1, HEADS, HEAD_DIM).astype(jnp.float32)
    near_values = near_pair[1].reshape(-1, HEADS, HEAD_DIM).astype(jnp.float32)
    far_keys = far_pair[0].reshape(blocks, -1, HEADS, HEAD_DIM).astype(jnp.float32)
    far_values = far_pair[1].reshape(blocks, -1, HEADS, HEAD_DIM).astype(jnp.float32)
    near_scores = jnp.einsum("bqhd,khd->bhqk", query_heads, near_keys) * scale
    near_scores = jnp.where(near_valid, near_scores, jnp.float32(-1e30))
    far_scores = jnp.einsum("bqhd,bkhd->bhqk", query_heads, far_keys) * scale
    far_scores = jnp.where(far_valid, far_scores, jnp.float32(-1e30))
    top_score = jnp.maximum(jnp.max(near_scores, -1), jnp.max(far_scores, -1))[..., None]
    near_exp = jnp.exp(near_scores - top_score)
    far_exp = jnp.exp(far_scores - top_score)
    total = jnp.sum(near_exp, -1) + jnp.sum(far_exp, -1)
    near_weights = lax.optimization_barrier(near_exp.astype(jnp.bfloat16)).astype(jnp.float32)
    far_weights = lax.optimization_barrier(far_exp.astype(jnp.bfloat16)).astype(jnp.float32)
    summed = jnp.einsum("bhqk,khd->bqhd", near_weights, near_values)
    summed = summed + jnp.einsum("bhqk,bkhd->bqhd", far_weights, far_values)
    attended = (summed / jnp.transpose(total, (0, 2, 1))[..., None]).reshape(blocks * BLK, D).astype(jnp.bfloat16)
    return jnp.dot(attended, out_weight, preferred_element_type=jnp.float32).astype(jnp.bfloat16)


def reference(queries, keys, values, far_picks, out_weight):
    blocks = TOK_DEV // BLK
    pair = jnp.stack([keys, values])
    padded = jnp.pad(pair, ((0, 0), (TOK_DEV, TOK_DEV), (0, 0)))
    offset_list = far_offsets()

    def one_device(device):
        start = (device * TOK_DEV).astype(jnp.int32)
        query_rows = lax.dynamic_slice_in_dim(queries, start, TOK_DEV, 0)
        near_pair = lax.dynamic_slice_in_dim(padded, start, 3 * TOK_DEV, 1)
        picks = lax.dynamic_slice_in_dim(far_picks, (device * blocks).astype(jnp.int32), blocks, 0)
        chosen_list = []
        valid_list = []
        for column in range(FAR):
            source = device + offset_list[column]
            usable = (source >= 0) & (source < N_TM)
            source_start = (jnp.clip(source, 0, N_TM - 1) * TOK_DEV).astype(jnp.int32)
            shard = lax.dynamic_slice_in_dim(pair, source_start, TOK_DEV, 1).reshape(2, blocks, BLK, D)
            chosen_list.append(jnp.take(shard, picks[:, column], axis=1))
            valid_list.append(usable)
        far_pair = jnp.stack(chosen_list, 2).reshape(2, blocks, FAR * BLK, D)
        far_valid = jnp.repeat(jnp.stack(valid_list), BLK)
        near_valid = jnp.repeat(jnp.stack([device > 0, jnp.array(True), device < N_TM - 1]), TOK_DEV)
        return attend(query_rows, near_pair, near_valid, far_pair, far_valid, out_weight)

    result = lax.map(one_device, jnp.arange(N_TM, dtype=jnp.int32))
    return result.reshape(TOKENS, D)
```

```python
import functools
import math

import jax
import jax.numpy as jnp
from jax import lax
from jax.experimental import pallas as pl
from jax.experimental.pallas import tpu as pltpu
from jax.sharding import PartitionSpec as P

HEAD_DIM = 128
BLK = 64
LEVELS = 2
PICKS = 2
FAR = 8
SCALE = HEAD_DIM ** (-0.5) * math.log2(math.e)
UNUSED = -1e30

VMEM = pl.BlockSpec(memory_space=pltpu.VMEM)
SMEM = pl.BlockSpec(memory_space=pltpu.SMEM)
ANY = pl.BlockSpec(memory_space=pl.ANY)
NT = (((1,), (1,)), ((), ()))


def column_offset(column):
    magnitude = 2 ** (1 + column // PICKS % LEVELS)
    return -magnitude if column < FAR // 2 else magnitude


def head_columns(head):
    return pl.ds(head * HEAD_DIM, HEAD_DIM)


def far_bias(picks_ref, device, offset, count, rows):
    usable = (device + offset >= 0) & (device + offset < count)
    lane = lax.broadcasted_iota(jnp.int32, (BLK, rows), 1)
    parts = []
    for block in range(rows // BLK):
        bias = jnp.full((BLK, rows), UNUSED, jnp.float32)
        for local in range(rows // BLK):
            named = jnp.int32(0)
            for column in range(FAR):
                hit = (picks_ref[block, column] == local) & (offset == column_offset(column))
                named = named + jnp.where(hit, 1, 0)
            named = jnp.where(usable, named, 0)
            value = jnp.where(named == 0, jnp.float32(UNUSED), (named - 1).astype(jnp.float32))
            bias = jnp.where(lane // BLK == local, value, bias)
        parts.append(bias)
    return jnp.concatenate(parts, axis=0)


def pack_kernel(keys_ref, values_ref, pair_ref, sems):
    first = pltpu.make_async_copy(keys_ref, pair_ref.at[0], sems.at[0])
    second = pltpu.make_async_copy(values_ref, pair_ref.at[1], sems.at[1])
    first.start()
    second.start()
    first.wait()
    second.wait()


def pack(keys, values):
    return pl.pallas_call(
        pack_kernel,
        out_shape=jax.ShapeDtypeStruct((2,) + keys.shape, keys.dtype),
        in_specs=[ANY, ANY],
        out_specs=VMEM,
        scratch_shapes=[pltpu.SemaphoreType.DMA((2,))],
        name="pack",
    )(keys, values)


def choose_kernel(index_ref, ends_ref, inner_ref, out_ref):
    place = lax.rem(index_ref[0], 4)
    ends = (place == 0) | (place == 3)

    @pl.when(ends)
    def _():
        out_ref[...] = ends_ref[...]

    @pl.when(jnp.logical_not(ends))
    def _():
        out_ref[...] = inner_ref[...]


def choose(index, ends, inner):
    return pl.pallas_call(
        choose_kernel,
        out_shape=jax.ShapeDtypeStruct(ends.shape, ends.dtype),
        in_specs=[SMEM, VMEM, VMEM],
        out_specs=VMEM,
        name="choose",
    )(index, ends, inner)


def first_kernel(
    count, index_ref, picks_ref, q_ref, own_ref, s0_ref, s1_ref, x1_ref, za_ref, zb_ref, acc_ref, top_ref, total_ref
):
    rows, width = q_ref.shape
    device = index_ref[0]
    sign = 1 - 2 * lax.rem(device, 2)
    shards = (own_ref, s0_ref, s1_ref, x1_ref, za_ref, zb_ref)
    outer = device - sign
    outer_bias = jnp.where((outer >= 0) & (outer < count), jnp.float32(0), jnp.float32(UNUSED))
    far = [far_bias(picks_ref, device, offset * sign, count, rows) for offset in (2, -4, 4)]
    for head in range(width // HEAD_DIM):
        cols = head_columns(head)
        queries = q_ref[:, cols]
        keys = jnp.concatenate([shard[0, :, cols] for shard in shards], axis=0)
        values = jnp.concatenate([shard[1, :, cols] for shard in shards], axis=0)
        scores = lax.dot_general(queries, keys, NT, preferred_element_type=jnp.float32) * SCALE
        parts = [scores[:, i * rows:(i + 1) * rows] for i in range(len(shards))]
        parts[2] = parts[2] + outer_bias
        for i in range(3):
            parts[3 + i] = parts[3 + i] + far[i]
        top = functools.reduce(jnp.maximum, parts)
        top = jnp.max(top, axis=1, keepdims=True)
        exps = [jnp.exp2(part - top) for part in parts]
        total = jnp.sum(functools.reduce(jnp.add, exps), axis=1, keepdims=True)
        weights = jnp.concatenate([e.astype(jnp.bfloat16) for e in exps], axis=1)
        acc_ref[:, cols] = jnp.dot(weights, values, preferred_element_type=jnp.float32)
        top_ref[head] = top
        total_ref[head] = total


def first(count, index, picks, queries, *shards):
    rows, width = queries.shape
    heads = width // HEAD_DIM
    column = jax.ShapeDtypeStruct((heads, rows, 1), jnp.float32)
    return pl.pallas_call(
        functools.partial(first_kernel, count),
        out_shape=(jax.ShapeDtypeStruct((rows, width), jnp.float32), column, column),
        in_specs=[SMEM, SMEM] + [VMEM] * 7,
        out_specs=(VMEM, VMEM, VMEM),
        compiler_params=pltpu.CompilerParams(vmem_limit_bytes=24 * 1024 * 1024),
        name="first",
    )(index, picks, queries, *shards)


def last_kernel(
    count, index_ref, picks_ref, q_ref, acc_ref, top_ref, total_ref, pair_ref, weight_ref, out_ref, attended_ref
):
    rows, width = q_ref.shape
    device = index_ref[0]
    sign = 1 - 2 * lax.rem(device, 2)
    bias = far_bias(picks_ref, device, -2 * sign, count, rows)
    for head in range(width // HEAD_DIM):
        cols = head_columns(head)
        scores = lax.dot_general(q_ref[:, cols], pair_ref[0, :, cols], NT, preferred_element_type=jnp.float32)
        scores = scores * SCALE + bias
        before = top_ref[head]
        top = jnp.maximum(before, jnp.max(scores, axis=1, keepdims=True))
        kept = jnp.exp2(before - top)
        exps = jnp.exp2(scores - top)
        total = total_ref[head] * kept + jnp.sum(exps, axis=1, keepdims=True)
        summed = acc_ref[:, cols] * kept + jnp.dot(
            exps.astype(jnp.bfloat16), pair_ref[1, :, cols], preferred_element_type=jnp.float32
        )
        attended_ref[:, cols] = (summed / total).astype(jnp.bfloat16)
    out_ref[...] = jnp.dot(attended_ref[...], weight_ref[...], preferred_element_type=jnp.float32).astype(jnp.bfloat16)


def last(count, index, picks, queries, acc, top, total, pair, weight):
    rows, width = queries.shape
    return pl.pallas_call(
        functools.partial(last_kernel, count),
        out_shape=jax.ShapeDtypeStruct((rows, width), jnp.bfloat16),
        in_specs=[SMEM, SMEM] + [VMEM] * 6,
        out_specs=VMEM,
        scratch_shapes=[pltpu.VMEM((rows, width), jnp.bfloat16)],
        compiler_params=pltpu.CompilerParams(vmem_limit_bytes=24 * 1024 * 1024),
        name="last",
    )(index, picks, queries, acc, top, total, pair, weight)


def moved(block, steps):
    count = lax.axis_size("tm")
    route = [(i, i + steps[i % 4]) for i in range(count)]
    return lax.ppermute(block, "tm", [(i, j) for i, j in route if 0 <= j < count])


def body(queries, keys, values, far_picks, out_weight):
    count = lax.axis_size("tm")
    index = lax.axis_index("tm").astype(jnp.int32).reshape(1)
    pair = pack(keys, values)
    x1 = moved(pair, (-2, 2, -2, 2))
    za = moved(pair, (4, -4, 4, -4))
    zb = moved(pair, (-4, 4, -4, 4))
    s0 = moved(pair, (1, -1, 1, -1))
    ahead = moved(choose(index, x1, s0), (4, 1, -1, -4))
    s1 = moved(x1, (1, -1, 1, -1))
    state = first(count, index, far_picks, queries, pair, s0, s1, x1, za, zb)
    return last(count, index, far_picks, queries, *state, ahead, out_weight)


def solution(mesh):
    placed = (
        P(("vid", "tm"), None),
        P(("vid", "tm"), None),
        P(("vid", "tm"), None),
        P(("vid", "tm"), None),
        P(),
    )
    return jax.shard_map(
        body, mesh=mesh, in_specs=placed, out_specs=P(("vid", "tm"), None), check_vma=False
    )
```

```python
import functools
import math

import jax
import jax.numpy as jnp
from jax import lax
from jax.experimental import pallas as pl
from jax.experimental.pallas import tpu as pltpu
from jax.sharding import PartitionSpec as P

HEAD_DIM = 128
BLK = 64
LEVELS = 2
PICKS = 2
FAR = 8
SCALE = HEAD_DIM ** (-0.5) * math.log2(math.e)
UNUSED = -1e30
LEAD = 2

VMEM = pl.BlockSpec(memory_space=pltpu.VMEM)
SMEM = pl.BlockSpec(memory_space=pltpu.SMEM)
ANY = pl.BlockSpec(memory_space=pl.ANY)
NT = (((1,), (1,)), ((), ()))


def column_offset(column):
    magnitude = 2 ** (1 + column // PICKS % LEVELS)
    return -magnitude if column < FAR // 2 else magnitude


def head_columns(head):
    return pl.ds(head * HEAD_DIM, HEAD_DIM)


def far_bias(picks_ref, device, offset, count, rows):
    usable = (device + offset >= 0) & (device + offset < count)
    lane = lax.broadcasted_iota(jnp.int32, (BLK, rows), 1)
    parts = []
    for block in range(rows // BLK):
        bias = jnp.full((BLK, rows), UNUSED, jnp.float32)
        for local in range(rows // BLK):
            named = jnp.int32(0)
            for column in range(FAR):
                hit = (picks_ref[block, column] == local) & (offset == column_offset(column))
                named = named + jnp.where(hit, 1, 0)
            named = jnp.where(usable, named, 0)
            value = jnp.where(named == 0, jnp.float32(UNUSED), (named - 1).astype(jnp.float32))
            bias = jnp.where(lane // BLK == local, value, bias)
        parts.append(bias)
    return jnp.concatenate(parts, axis=0)


def pack_kernel(keys_ref, values_ref, pair_ref, sems):
    first = pltpu.make_async_copy(keys_ref, pair_ref.at[0], sems.at[0])
    second = pltpu.make_async_copy(values_ref, pair_ref.at[1], sems.at[1])
    first.start()
    second.start()
    first.wait()
    second.wait()


def pack(keys, values):
    return pl.pallas_call(
        pack_kernel,
        out_shape=jax.ShapeDtypeStruct((2,) + keys.shape, keys.dtype),
        in_specs=[ANY, ANY],
        out_specs=VMEM,
        scratch_shapes=[pltpu.SemaphoreType.DMA((2,))],
        compiler_params=pltpu.CompilerParams(vmem_limit_bytes=4 * 1024 * 1024),
        name="pack",
    )(keys, values)


def choose_kernel(index_ref, ends_ref, inner_ref, out_ref):
    place = lax.rem(index_ref[0], 4)
    ends = (place == 0) | (place == 3)

    @pl.when(ends)
    def _():
        out_ref[...] = ends_ref[...]

    @pl.when(jnp.logical_not(ends))
    def _():
        out_ref[...] = inner_ref[...]


def choose(index, ends, inner):
    return pl.pallas_call(
        choose_kernel,
        out_shape=jax.ShapeDtypeStruct(ends.shape, ends.dtype),
        in_specs=[SMEM, VMEM, VMEM],
        out_specs=VMEM,
        compiler_params=pltpu.CompilerParams(vmem_limit_bytes=4 * 1024 * 1024),
        name="choose",
    )(index, ends, inner)


def staged(heads, score, soften, gather):
    for step in range(heads + 2 * LEAD):
        if step < heads:
            score(step)
        if 0 <= step - LEAD < heads:
            soften(step - LEAD)
        if 0 <= step - 2 * LEAD < heads:
            gather(step - 2 * LEAD)


def first_kernel(
    count, index_ref, picks_ref, q_ref, own_ref, s0_ref, s1_ref, x1_ref, za_ref, zb_ref, acc_ref, top_ref, total_ref
):
    rows, width = q_ref.shape
    device = index_ref[0]
    sign = 1 - 2 * lax.rem(device, 2)
    shards = (own_ref, s0_ref, s1_ref, x1_ref, za_ref, zb_ref)
    outer = device - sign
    outer_bias = jnp.where((outer >= 0) & (outer < count), jnp.float32(0), jnp.float32(UNUSED))
    far = [far_bias(picks_ref, device, offset * sign, count, rows) for offset in (2, -4, 4)]
    scores, weights = {}, {}

    def score(head):
        cols = head_columns(head)
        keys = jnp.concatenate([shard[0, :, cols] for shard in shards], axis=0)
        scores[head] = lax.dot_general(q_ref[:, cols], keys, NT, preferred_element_type=jnp.float32)

    def soften(head):
        scaled = scores.pop(head) * SCALE
        parts = [scaled[:, i * rows:(i + 1) * rows] for i in range(len(shards))]
        parts[2] = parts[2] + outer_bias
        for i in range(3):
            parts[3 + i] = parts[3 + i] + far[i]
        top = jnp.max(functools.reduce(jnp.maximum, parts), axis=1, keepdims=True)
        exps = [jnp.exp2(part - top) for part in parts]
        total = jnp.sum(functools.reduce(jnp.add, exps), axis=1, keepdims=True)
        weights[head] = jnp.concatenate([e.astype(jnp.bfloat16) for e in exps], axis=1)
        top_ref[head] = jnp.broadcast_to(top, top_ref.shape[1:])
        total_ref[head] = jnp.broadcast_to(total, total_ref.shape[1:])

    def gather(head):
        cols = head_columns(head)
        values = jnp.concatenate([shard[1, :, cols] for shard in shards], axis=0)
        acc_ref[:, cols] = jnp.dot(weights.pop(head), values, preferred_element_type=jnp.float32)

    staged(width // HEAD_DIM, score, soften, gather)


def first(count, index, picks, queries, *shards):
    rows, width = queries.shape
    heads = width // HEAD_DIM
    column = jax.ShapeDtypeStruct((heads, rows, HEAD_DIM), jnp.float32)
    return pl.pallas_call(
        functools.partial(first_kernel, count),
        out_shape=(jax.ShapeDtypeStruct((rows, width), jnp.float32), column, column),
        in_specs=[SMEM, SMEM] + [VMEM] * 7,
        out_specs=(VMEM, VMEM, VMEM),
        compiler_params=pltpu.CompilerParams(vmem_limit_bytes=16 * 1024 * 1024),
        name="first",
    )(index, picks, queries, *shards)


def last_kernel(
    count, index_ref, picks_ref, q_ref, acc_ref, top_ref, total_ref, pair_ref, weight_ref, out_ref, attended_ref
):
    rows, width = q_ref.shape
    device = index_ref[0]
    sign = 1 - 2 * lax.rem(device, 2)
    bias = far_bias(picks_ref, device, -2 * sign, count, rows)
    scores, state = {}, {}

    def score(head):
        cols = head_columns(head)
        scores[head] = lax.dot_general(q_ref[:, cols], pair_ref[0, :, cols], NT, preferred_element_type=jnp.float32)

    def soften(head):
        scaled = scores.pop(head) * SCALE + bias
        before = top_ref[head]
        top = jnp.maximum(before, jnp.max(scaled, axis=1, keepdims=True))
        kept = jnp.exp2(before - top)
        exps = jnp.exp2(scaled - top)
        total = total_ref[head] * kept + jnp.sum(exps, axis=1, keepdims=True)
        state[head] = (kept, total, exps.astype(jnp.bfloat16))

    def gather(head):
        cols = head_columns(head)
        kept, total, weights = state.pop(head)
        summed = jnp.dot(weights, pair_ref[1, :, cols], preferred_element_type=jnp.float32)
        attended_ref[:, cols] = ((acc_ref[:, cols] * kept + summed) / total).astype(jnp.bfloat16)

    staged(width // HEAD_DIM, score, soften, gather)
    out_ref[...] = jnp.dot(attended_ref[...], weight_ref[...], preferred_element_type=jnp.float32).astype(jnp.bfloat16)


def last(count, index, picks, queries, acc, top, total, pair, weight):
    rows, width = queries.shape
    return pl.pallas_call(
        functools.partial(last_kernel, count),
        out_shape=jax.ShapeDtypeStruct((rows, width), jnp.bfloat16),
        in_specs=[SMEM, SMEM] + [VMEM] * 6,
        out_specs=VMEM,
        scratch_shapes=[pltpu.VMEM((rows, width), jnp.bfloat16)],
        compiler_params=pltpu.CompilerParams(vmem_limit_bytes=16 * 1024 * 1024),
        name="last",
    )(index, picks, queries, acc, top, total, pair, weight)


def moved(block, steps):
    count = lax.axis_size("tm")
    route = [(i, i + steps[i % 4]) for i in range(count)]
    return lax.ppermute(block, "tm", [(i, j) for i, j in route if 0 <= j < count])


def body(queries, keys, values, far_picks, out_weight):
    count = lax.axis_size("tm")
    index = lax.axis_index("tm").astype(jnp.int32).reshape(1)
    pair = pack(keys, values)
    x1 = moved(pair, (-2, 2, -2, 2))
    za = moved(pair, (4, -4, 4, -4))
    zb = moved(pair, (-4, 4, -4, 4))
    s0 = moved(pair, (1, -1, 1, -1))
    ahead = moved(choose(index, x1, s0), (4, 1, -1, -4))
    s1 = moved(x1, (1, -1, 1, -1))
    state = first(count, index, far_picks, queries, pair, s0, s1, x1, za, zb)
    return last(count, index, far_picks, queries, *state, ahead, out_weight)


def solution(mesh):
    placed = (
        P(("vid", "tm"), None),
        P(("vid", "tm"), None),
        P(("vid", "tm"), None),
        P(("vid", "tm"), None),
        P(),
    )
    return jax.shard_map(
        body, mesh=mesh, in_specs=placed, out_specs=P(("vid", "tm"), None), check_vma=False
    )
```

```python
import functools
import math

import jax
import jax.numpy as jnp
from jax import lax
from jax.experimental import pallas as pl
from jax.experimental.pallas import tpu as pltpu
from jax.sharding import PartitionSpec as P

HEAD_DIM = 128
BLK = 64
LEVELS = 2
PICKS = 2
FAR = 8
SCALE = HEAD_DIM ** (-0.5) * math.log2(math.e)
UNUSED = -1e30
LEAD = 2
NONE = 1 << 20

STEPS = ((-4, 1, -1, 4), (4, 4, -4, -4), (3, -4, 4, -3))
SIDE_STEPS = (2, 0, 0, -2)
RELAY_STEPS = (0, 3, -3, 0)
SWAP_STEPS = (1, -1, 1, -1)
FIRST_OFFSETS = ((4, 1, -1, -4),)
SECOND_OFFSETS = ((-4, -4, 4, 4), (NONE, 2, -2, NONE))
MIDDLE_OFFSETS = ((-1, 4, -4, 1),)
LAST_OFFSETS = ((2, -2, 2, -2), (-2, NONE, NONE, 2))

VMEM = pl.BlockSpec(memory_space=pltpu.VMEM)
SMEM = pl.BlockSpec(memory_space=pltpu.SMEM)
ANY = pl.BlockSpec(memory_space=pl.ANY)
NT = (((1,), (1,)), ((), ()))


def after_kernel(block_ref, before_ref, out_ref):
    out_ref[...] = block_ref[...]


def after(block, before, flops):
    return pl.pallas_call(
        after_kernel,
        out_shape=jax.ShapeDtypeStruct(block.shape, block.dtype),
        in_specs=[VMEM, VMEM],
        out_specs=VMEM,
        cost_estimate=pl.CostEstimate(flops=flops, bytes_accessed=0, transcendentals=0),
        compiler_params=pltpu.CompilerParams(vmem_limit_bytes=4 * 1024 * 1024),
        name="after",
    )(block, before)


def column_offset(column):
    magnitude = 2 ** (1 + column // PICKS % LEVELS)
    return -magnitude if column < FAR // 2 else magnitude


def head_columns(head):
    return pl.ds(head * HEAD_DIM, HEAD_DIM)


def by_place(device, choices):
    place = lax.rem(device, 4)
    value = jnp.int32(choices[0])
    for i in range(1, 4):
        value = jnp.where(place == i, jnp.int32(choices[i]), value)
    return value


def shard_bias(picks_ref, device, offset, count, rows):
    usable = (device + offset >= 0) & (device + offset < count)
    near = (offset >= -1) & (offset <= 1)
    lane = lax.broadcasted_iota(jnp.int32, (BLK, rows), 1)
    parts = []
    for block in range(rows // BLK):
        bias = jnp.full((BLK, rows), UNUSED, jnp.float32)
        for local in range(rows // BLK):
            named = jnp.where(near, 1, 0)
            for column in range(FAR):
                hit = (picks_ref[block, column] == local) & (offset == column_offset(column))
                named = named + jnp.where(hit, 1, 0)
            named = jnp.where(usable, named, 0)
            value = jnp.where(named == 0, jnp.float32(UNUSED), (named - 1).astype(jnp.float32))
            bias = jnp.where(lane // BLK == local, value, bias)
        parts.append(bias)
    return jnp.concatenate(parts, axis=0)


def pack_kernel(keys_ref, values_ref, pair_ref, sems):
    first = pltpu.make_async_copy(keys_ref, pair_ref.at[0], sems.at[0])
    second = pltpu.make_async_copy(values_ref, pair_ref.at[1], sems.at[1])
    first.start()
    second.start()
    first.wait()
    second.wait()


def pack(keys, values):
    return pl.pallas_call(
        pack_kernel,
        out_shape=jax.ShapeDtypeStruct((2,) + keys.shape, keys.dtype),
        in_specs=[ANY, ANY],
        out_specs=VMEM,
        scratch_shapes=[pltpu.SemaphoreType.DMA((2,))],
        compiler_params=pltpu.CompilerParams(vmem_limit_bytes=4 * 1024 * 1024),
        name="pack",
    )(keys, values)


def choose_kernel(index_ref, ends_ref, inner_ref, out_ref):
    place = lax.rem(index_ref[0], 4)
    ends = (place == 0) | (place == 3)

    @pl.when(ends)
    def _():
        out_ref[...] = ends_ref[...]

    @pl.when(jnp.logical_not(ends))
    def _():
        out_ref[...] = inner_ref[...]


def choose(index, ends, inner):
    return pl.pallas_call(
        choose_kernel,
        out_shape=jax.ShapeDtypeStruct(ends.shape, ends.dtype),
        in_specs=[SMEM, VMEM, VMEM],
        out_specs=VMEM,
        compiler_params=pltpu.CompilerParams(vmem_limit_bytes=4 * 1024 * 1024),
        name="choose",
    )(index, ends, inner)


def staged(heads, score, soften, gather):
    for step in range(heads + 2 * LEAD):
        if step < heads:
            score(step)
        if 0 <= step - LEAD < heads:
            soften(step - LEAD)
        if 0 <= step - 2 * LEAD < heads:
            gather(step - 2 * LEAD)


def attend(q_ref, shards, biases, top_ref, total_ref, finish):
    rows, width = q_ref.shape
    scores, state = {}, {}

    def part(which, cols):
        return jnp.concatenate([shard[which, :, cols] for shard in shards], axis=0)

    def score(head):
        cols = head_columns(head)
        scores[head] = lax.dot_general(q_ref[:, cols], part(0, cols), NT, preferred_element_type=jnp.float32)

    def soften(head):
        scaled = scores.pop(head) * SCALE
        parts = [scaled[:, i * rows:(i + 1) * rows] for i in range(len(shards))]
        parts = [p if bias is None else p + bias for p, bias in zip(parts, biases)]
        top = jnp.max(functools.reduce(jnp.maximum, parts), axis=1, keepdims=True)
        kept = None
        if top_ref is not None:
            before = top_ref[head]
            top = jnp.maximum(before, top)
            kept = jnp.exp2(before - top)
        exps = [jnp.exp2(p - top) for p in parts]
        total = jnp.sum(functools.reduce(jnp.add, exps), axis=1, keepdims=True)
        if top_ref is not None:
            total = total_ref[head] * kept + total
        state[head] = (top, kept, total, jnp.concatenate([e.astype(jnp.bfloat16) for e in exps], axis=1))

    def gather(head):
        top, kept, total, weights = state.pop(head)
        summed = jnp.dot(weights, part(1, head_columns(head)), preferred_element_type=jnp.float32)
        finish(head, top, kept, total, summed)

    staged(width // HEAD_DIM, score, soften, gather)


def first_kernel(
    count, index_ref, picks_ref, q_ref, own_ref, mate_ref, one_ref, weight_ref, acc_ref, top_ref,
    total_ref, held_ref, sem
):
    fetch = pltpu.make_async_copy(weight_ref, held_ref, sem)
    fetch.start()
    rows = q_ref.shape[0]
    device = index_ref[0]
    offsets = FIRST_OFFSETS
    biases = [shard_bias(picks_ref, device, by_place(device, offset), count, rows) for offset in offsets]

    def finish(head, top, kept, total, summed):
        acc_ref[:, head_columns(head)] = summed
        top_ref[head] = jnp.broadcast_to(top, top_ref.shape[1:])
        total_ref[head] = jnp.broadcast_to(total, total_ref.shape[1:])

    attend(q_ref, (own_ref, mate_ref, one_ref), [None, None] + biases, None, None, finish)
    fetch.wait()


def first(count, index, picks, queries, weight, *shards):
    rows, width = queries.shape
    column = jax.ShapeDtypeStruct((width // HEAD_DIM, rows, HEAD_DIM), jnp.float32)
    return pl.pallas_call(
        functools.partial(first_kernel, count),
        out_shape=(jax.ShapeDtypeStruct((rows, width), jnp.float32), column, column,
                   jax.ShapeDtypeStruct(weight.shape, weight.dtype)),
        in_specs=[SMEM, SMEM] + [VMEM] * (1 + len(shards)) + [ANY],
        out_specs=(VMEM, VMEM, VMEM, VMEM),
        scratch_shapes=[pltpu.SemaphoreType.DMA],
        compiler_params=pltpu.CompilerParams(vmem_limit_bytes=16 * 1024 * 1024),
        name="first",
    )(index, picks, queries, *shards, weight)


def middle_kernel(count, offsets, index_ref, picks_ref, q_ref, acc_ref, top_ref, total_ref, *refs):
    shard_refs = refs[:len(offsets)]
    new_acc_ref, new_top_ref, new_total_ref = refs[len(offsets):]
    rows = q_ref.shape[0]
    device = index_ref[0]
    biases = [shard_bias(picks_ref, device, by_place(device, offset), count, rows) for offset in offsets]

    def finish(head, top, kept, total, summed):
        cols = head_columns(head)
        new_acc_ref[:, cols] = acc_ref[:, cols] * kept + summed
        new_top_ref[head] = top
        new_total_ref[head] = total

    attend(q_ref, shard_refs, biases, top_ref, total_ref, finish)


def middle(count, offsets, index, picks, queries, acc, top, total, *shards):
    return pl.pallas_call(
        functools.partial(middle_kernel, count, offsets),
        out_shape=[jax.ShapeDtypeStruct(x.shape, x.dtype) for x in (acc, top, total)],
        in_specs=[SMEM, SMEM] + [VMEM] * (4 + len(shards)),
        out_specs=[VMEM, VMEM, VMEM],
        compiler_params=pltpu.CompilerParams(vmem_limit_bytes=16 * 1024 * 1024),
        name="middle",
    )(index, picks, queries, acc, top, total, *shards)


def last_kernel(
    count, index_ref, picks_ref, q_ref, acc_ref, top_ref, total_ref, swap_ref, relay_ref, weight_ref, out_ref,
    attended_ref
):
    rows = q_ref.shape[0]
    device = index_ref[0]
    biases = [shard_bias(picks_ref, device, by_place(device, offset), count, rows) for offset in LAST_OFFSETS]

    def finish(head, top, kept, total, summed):
        cols = head_columns(head)
        attended_ref[:, cols] = ((acc_ref[:, cols] * kept + summed) / total).astype(jnp.bfloat16)

    attend(q_ref, (swap_ref, relay_ref), biases, top_ref, total_ref, finish)
    out_ref[...] = jnp.dot(attended_ref[...], weight_ref[...], preferred_element_type=jnp.float32).astype(jnp.bfloat16)


def last(count, index, picks, queries, acc, top, total, *rest):
    rows, width = queries.shape
    return pl.pallas_call(
        functools.partial(last_kernel, count),
        out_shape=jax.ShapeDtypeStruct((rows, width), jnp.bfloat16),
        in_specs=[SMEM, SMEM] + [VMEM] * (4 + len(rest)),
        out_specs=VMEM,
        scratch_shapes=[pltpu.VMEM((rows, width), jnp.bfloat16)],
        compiler_params=pltpu.CompilerParams(vmem_limit_bytes=16 * 1024 * 1024),
        name="last",
    )(index, picks, queries, acc, top, total, *rest)


def moved(block, steps):
    count = lax.axis_size("tm")
    route = [(i, i + steps[i % 4]) for i in range(count) if steps[i % 4]]
    return lax.ppermute(block, "tm", [(i, j) for i, j in route if 0 <= j < count])


def body(queries, keys, values, far_picks, out_weight):
    count = lax.axis_size("tm")
    index = lax.axis_index("tm").astype(jnp.int32).reshape(1)
    pair = jnp.stack([keys, values])
    one = moved(pair, STEPS[0])
    two = moved(pair, STEPS[1])
    side = moved(pair, SIDE_STEPS)
    three = moved(choose(index, one, pair), STEPS[2])
    relay = after(moved(one, RELAY_STEPS), two, 10000000000)
    swap = moved(choose(index, three, one), SWAP_STEPS)
    mate = moved(pair, SWAP_STEPS)
    *state, held = first(count, index, far_picks, queries, out_weight, pair, mate, one)
    state = middle(count, SECOND_OFFSETS, index, far_picks, queries, *state, two, side)
    state = middle(count, MIDDLE_OFFSETS, index, far_picks, queries, *state, three)
    return last(count, index, far_picks, queries, *state, swap, relay, held)


def solution(mesh):
    placed = (
        P(("vid", "tm"), None),
        P(("vid", "tm"), None),
        P(("vid", "tm"), None),
        P(("vid", "tm"), None),
        P(),
    )
    return jax.shard_map(
        body, mesh=mesh, in_specs=placed, out_specs=P(("vid", "tm"), None), check_vma=False
    )
```

```python
import functools
import math

import jax
import jax.numpy as jnp
from jax import lax
from jax.experimental import pallas as pl
from jax.experimental.pallas import tpu as pltpu
from jax.sharding import PartitionSpec as P

HEAD_DIM = 128
BLK = 64
LEVELS = 2
PICKS = 2
FAR = 8
SCALE = HEAD_DIM ** (-0.5) * math.log2(math.e)
UNUSED = -1e30
LEAD = 2
NONE = 1 << 20

STEPS = ((-4, 1, -1, 4), (4, 4, -4, -4), (3, -4, 4, -3))
SIDE_STEPS = (2, 0, 0, -2)
RELAY_STEPS = (0, 3, -3, 0)
SWAP_STEPS = (1, -1, 1, -1)
FIRST_OFFSETS = ((4, 1, -1, -4),)
LATER_OFFSETS = (
    (-4, -4, 4, 4), (NONE, 2, -2, NONE),
    (-1, 4, -4, 1),
    (2, -2, 2, -2), (-2, NONE, NONE, 2),
)

VMEM = pl.BlockSpec(memory_space=pltpu.VMEM)
SMEM = pl.BlockSpec(memory_space=pltpu.SMEM)
ANY = pl.BlockSpec(memory_space=pl.ANY)
NT = (((1,), (1,)), ((), ()))


def after_kernel(block_ref, before_ref, out_ref):
    out_ref[...] = block_ref[...]


def after(block, before, flops):
    return pl.pallas_call(
        after_kernel,
        out_shape=jax.ShapeDtypeStruct(block.shape, block.dtype),
        in_specs=[VMEM, VMEM],
        out_specs=VMEM,
        cost_estimate=pl.CostEstimate(flops=flops, bytes_accessed=0, transcendentals=0),
        compiler_params=pltpu.CompilerParams(vmem_limit_bytes=4 * 1024 * 1024),
        name="after",
    )(block, before)


def column_offset(column):
    magnitude = 2 ** (1 + column // PICKS % LEVELS)
    return -magnitude if column < FAR // 2 else magnitude


def head_columns(head):
    return pl.ds(head * HEAD_DIM, HEAD_DIM)


def by_place(device, choices):
    place = lax.rem(device, 4)
    value = jnp.int32(choices[0])
    for i in range(1, 4):
        value = jnp.where(place == i, jnp.int32(choices[i]), value)
    return value


def shard_bias(picks_ref, device, offset, count, rows):
    usable = (device + offset >= 0) & (device + offset < count)
    near = (offset >= -1) & (offset <= 1)
    lane = lax.broadcasted_iota(jnp.int32, (BLK, rows), 1)
    parts = []
    for block in range(rows // BLK):
        bias = jnp.full((BLK, rows), UNUSED, jnp.float32)
        for local in range(rows // BLK):
            named = jnp.where(near, 1, 0)
            for column in range(FAR):
                hit = (picks_ref[block, column] == local) & (offset == column_offset(column))
                named = named + jnp.where(hit, 1, 0)
            named = jnp.where(usable, named, 0)
            value = jnp.where(named == 0, jnp.float32(UNUSED), (named - 1).astype(jnp.float32))
            bias = jnp.where(lane // BLK == local, value, bias)
        parts.append(bias)
    return jnp.concatenate(parts, axis=0)


def pack_kernel(keys_ref, values_ref, pair_ref, sems):
    first = pltpu.make_async_copy(keys_ref, pair_ref.at[0], sems.at[0])
    second = pltpu.make_async_copy(values_ref, pair_ref.at[1], sems.at[1])
    first.start()
    second.start()
    first.wait()
    second.wait()


def pack(keys, values):
    return pl.pallas_call(
        pack_kernel,
        out_shape=jax.ShapeDtypeStruct((2,) + keys.shape, keys.dtype),
        in_specs=[ANY, ANY],
        out_specs=VMEM,
        scratch_shapes=[pltpu.SemaphoreType.DMA((2,))],
        compiler_params=pltpu.CompilerParams(vmem_limit_bytes=4 * 1024 * 1024),
        name="pack",
    )(keys, values)


def choose_kernel(index_ref, ends_ref, inner_ref, out_ref):
    place = lax.rem(index_ref[0], 4)
    ends = (place == 0) | (place == 3)

    @pl.when(ends)
    def _():
        out_ref[...] = ends_ref[...]

    @pl.when(jnp.logical_not(ends))
    def _():
        out_ref[...] = inner_ref[...]


def choose(index, ends, inner):
    return pl.pallas_call(
        choose_kernel,
        out_shape=jax.ShapeDtypeStruct(ends.shape, ends.dtype),
        in_specs=[SMEM, VMEM, VMEM],
        out_specs=VMEM,
        compiler_params=pltpu.CompilerParams(vmem_limit_bytes=4 * 1024 * 1024),
        name="choose",
    )(index, ends, inner)


def staged(heads, score, soften, gather):
    for step in range(heads + 2 * LEAD):
        if step < heads:
            score(step)
        if 0 <= step - LEAD < heads:
            soften(step - LEAD)
        if 0 <= step - 2 * LEAD < heads:
            gather(step - 2 * LEAD)


def attend(q_ref, shards, biases, top_ref, total_ref, finish):
    rows, width = q_ref.shape
    scores, state = {}, {}

    def part(which, cols):
        return jnp.concatenate([shard[which, :, cols] for shard in shards], axis=0)

    def score(head):
        cols = head_columns(head)
        scores[head] = lax.dot_general(q_ref[:, cols], part(0, cols), NT, preferred_element_type=jnp.float32)

    def soften(head):
        scaled = scores.pop(head) * SCALE
        parts = [scaled[:, i * rows:(i + 1) * rows] for i in range(len(shards))]
        parts = [p if bias is None else p + bias for p, bias in zip(parts, biases)]
        top = jnp.max(functools.reduce(jnp.maximum, parts), axis=1, keepdims=True)
        kept = None
        if top_ref is not None:
            before = top_ref[head]
            top = jnp.maximum(before, top)
            kept = jnp.exp2(before - top)
        exps = [jnp.exp2(p - top) for p in parts]
        total = jnp.sum(functools.reduce(jnp.add, exps), axis=1, keepdims=True)
        if top_ref is not None:
            total = total_ref[head] * kept + total
        state[head] = (top, kept, total, jnp.concatenate([e.astype(jnp.bfloat16) for e in exps], axis=1))

    def gather(head):
        top, kept, total, weights = state.pop(head)
        summed = jnp.dot(weights, part(1, head_columns(head)), preferred_element_type=jnp.float32)
        finish(head, top, kept, total, summed)

    staged(width // HEAD_DIM, score, soften, gather)


def first_kernel(
    count, index_ref, picks_ref, q_ref, own_ref, mate_ref, one_ref, weight_ref, acc_ref, top_ref,
    total_ref, held_ref, later_ref, sem
):
    fetch = pltpu.make_async_copy(weight_ref, held_ref, sem)
    fetch.start()
    rows = q_ref.shape[0]
    device = index_ref[0]
    biases = [shard_bias(picks_ref, device, by_place(device, offset), count, rows) for offset in FIRST_OFFSETS]
    for i, offset in enumerate(LATER_OFFSETS):
        later_ref[i] = shard_bias(picks_ref, device, by_place(device, offset), count, rows)

    def finish(head, top, kept, total, summed):
        acc_ref[:, head_columns(head)] = summed
        top_ref[head] = jnp.broadcast_to(top, top_ref.shape[1:])
        total_ref[head] = jnp.broadcast_to(total, total_ref.shape[1:])

    attend(q_ref, (own_ref, mate_ref, one_ref), [None, None] + biases, None, None, finish)
    fetch.wait()


def first(count, index, picks, queries, weight, *shards):
    rows, width = queries.shape
    column = jax.ShapeDtypeStruct((width // HEAD_DIM, rows, HEAD_DIM), jnp.float32)
    return pl.pallas_call(
        functools.partial(first_kernel, count),
        out_shape=(jax.ShapeDtypeStruct((rows, width), jnp.float32), column, column,
                   jax.ShapeDtypeStruct(weight.shape, weight.dtype),
                   jax.ShapeDtypeStruct((len(LATER_OFFSETS), rows, rows), jnp.float32)),
        in_specs=[SMEM, SMEM] + [VMEM] * (1 + len(shards)) + [ANY],
        out_specs=(VMEM, VMEM, VMEM, VMEM, VMEM),
        scratch_shapes=[pltpu.SemaphoreType.DMA],
        compiler_params=pltpu.CompilerParams(vmem_limit_bytes=16 * 1024 * 1024),
        name="first",
    )(index, picks, queries, *shards, weight)


def middle_kernel(places, bias_ref, q_ref, acc_ref, top_ref, total_ref, *refs):
    shard_refs = refs[:len(places)]
    new_acc_ref, new_top_ref, new_total_ref = refs[len(places):]

    def finish(head, top, kept, total, summed):
        cols = head_columns(head)
        new_acc_ref[:, cols] = acc_ref[:, cols] * kept + summed
        new_top_ref[head] = top
        new_total_ref[head] = total

    attend(q_ref, shard_refs, [bias_ref[i] for i in places], top_ref, total_ref, finish)


def middle(places, bias, queries, acc, top, total, *shards):
    return pl.pallas_call(
        functools.partial(middle_kernel, places),
        out_shape=[jax.ShapeDtypeStruct(x.shape, x.dtype) for x in (acc, top, total)],
        in_specs=[VMEM] * (5 + len(shards)),
        out_specs=[VMEM, VMEM, VMEM],
        compiler_params=pltpu.CompilerParams(vmem_limit_bytes=16 * 1024 * 1024),
        name="middle",
    )(bias, queries, acc, top, total, *shards)


def last_kernel(
    places, bias_ref, q_ref, acc_ref, top_ref, total_ref, swap_ref, relay_ref, weight_ref, out_ref,
    attended_ref
):
    def finish(head, top, kept, total, summed):
        cols = head_columns(head)
        attended_ref[:, cols] = ((acc_ref[:, cols] * kept + summed) / total).astype(jnp.bfloat16)

    attend(q_ref, (swap_ref, relay_ref), [bias_ref[i] for i in places], top_ref, total_ref, finish)
    out_ref[...] = jnp.dot(attended_ref[...], weight_ref[...], preferred_element_type=jnp.float32).astype(jnp.bfloat16)


def last(places, bias, queries, acc, top, total, *rest):
    rows, width = queries.shape
    return pl.pallas_call(
        functools.partial(last_kernel, places),
        out_shape=jax.ShapeDtypeStruct((rows, width), jnp.bfloat16),
        in_specs=[VMEM] * (5 + len(rest)),
        out_specs=VMEM,
        scratch_shapes=[pltpu.VMEM((rows, width), jnp.bfloat16)],
        compiler_params=pltpu.CompilerParams(vmem_limit_bytes=16 * 1024 * 1024),
        name="last",
    )(bias, queries, acc, top, total, *rest)


def moved(block, steps):
    count = lax.axis_size("tm")
    route = [(i, i + steps[i % 4]) for i in range(count) if steps[i % 4]]
    return lax.ppermute(block, "tm", [(i, j) for i, j in route if 0 <= j < count])


def body(queries, keys, values, far_picks, out_weight):
    count = lax.axis_size("tm")
    index = lax.axis_index("tm").astype(jnp.int32).reshape(1)
    pair = jnp.stack([keys, values])
    one = moved(pair, STEPS[0])
    two = moved(pair, STEPS[1])
    side = moved(pair, SIDE_STEPS)
    three = moved(choose(index, one, pair), STEPS[2])
    relay = after(moved(one, RELAY_STEPS), two, 10000000000)
    swap = moved(choose(index, three, one), SWAP_STEPS)
    mate = moved(pair, SWAP_STEPS)
    *state, held, bias = first(count, index, far_picks, queries, out_weight, pair, mate, one)
    state = middle((0, 1), bias, queries, *state, two, side)
    state = middle((2,), bias, queries, *state, three)
    return last((3, 4), bias, queries, *state, swap, relay, held)


def solution(mesh):
    placed = (
        P(("vid", "tm"), None),
        P(("vid", "tm"), None),
        P(("vid", "tm"), None),
        P(("vid", "tm"), None),
        P(),
    )
    return jax.shard_map(
        body, mesh=mesh, in_specs=placed, out_specs=P(("vid", "tm"), None), check_vma=False
    )
```

```python
import functools
import math

import jax
import jax.numpy as jnp
from jax import lax
from jax.experimental import pallas as pl
from jax.experimental.pallas import tpu as pltpu
from jax.sharding import PartitionSpec as P

HEAD_DIM = 128
BLK = 64
LEVELS = 2
PICKS = 2
FAR = 8
SCALE = HEAD_DIM ** (-0.5) * math.log2(math.e)
UNUSED = -1e30
LEAD = 4
NONE = 1 << 20

STEPS = ((-4, 1, -1, 4), (4, 4, -4, -4), (3, -4, 4, -3))
RELAYED = (4, 0, 0, -4)
SIDE_STEPS = (2, 0, 0, -2)
RELAY_STEPS = (0, 3, -3, 0)
SWAP_STEPS = (1, -1, 1, -1)
FIRST_OFFSETS = ((4, 1, -1, -4),)
LATER_OFFSETS = (
    (-4, -4, 4, 4), (NONE, 2, -2, NONE),
    (-1, 4, -4, 1),
    (2, -2, 2, -2), (-2, NONE, NONE, 2),
)

VMEM = pl.BlockSpec(memory_space=pltpu.VMEM)
SMEM = pl.BlockSpec(memory_space=pltpu.SMEM)
ANY = pl.BlockSpec(memory_space=pl.ANY)
NT = (((1,), (1,)), ((), ()))


def after_kernel(block_ref, out_ref):
    out_ref[...] = block_ref[...]


def after(block, flops):
    return pl.pallas_call(
        after_kernel,
        out_shape=jax.ShapeDtypeStruct(block.shape, block.dtype),
        in_specs=[VMEM],
        out_specs=VMEM,
        cost_estimate=pl.CostEstimate(flops=flops, bytes_accessed=0, transcendentals=0),
        compiler_params=pltpu.CompilerParams(vmem_limit_bytes=4 * 1024 * 1024),
        name="after",
    )(block)


def column_offset(column):
    magnitude = 2 ** (1 + column // PICKS % LEVELS)
    return -magnitude if column < FAR // 2 else magnitude


def head_columns(head):
    return pl.ds(head * HEAD_DIM, HEAD_DIM)


def by_place(device, choices):
    place = lax.rem(device, 4)
    value = jnp.int32(choices[0])
    for i in range(1, 4):
        value = jnp.where(place == i, jnp.int32(choices[i]), value)
    return value


def shard_bias(picks_ref, device, offset, count, rows):
    usable = (device + offset >= 0) & (device + offset < count)
    near = (offset >= -1) & (offset <= 1)
    lane = lax.broadcasted_iota(jnp.int32, (BLK, rows), 1)
    parts = []
    for block in range(rows // BLK):
        bias = jnp.full((BLK, rows), UNUSED, jnp.float32)
        for local in range(rows // BLK):
            named = jnp.where(near, 1, 0)
            for column in range(FAR):
                hit = (picks_ref[block, column] == local) & (offset == column_offset(column))
                named = named + jnp.where(hit, 1, 0)
            named = jnp.where(usable, named, 0)
            value = jnp.where(named == 0, jnp.float32(UNUSED), (named - 1).astype(jnp.float32))
            bias = jnp.where(lane // BLK == local, value, bias)
        parts.append(bias)
    return jnp.concatenate(parts, axis=0)


def pack_kernel(keys_ref, values_ref, pair_ref, sems):
    first = pltpu.make_async_copy(keys_ref, pair_ref.at[0], sems.at[0])
    second = pltpu.make_async_copy(values_ref, pair_ref.at[1], sems.at[1])
    first.start()
    second.start()
    first.wait()
    second.wait()


def pack(keys, values):
    return pl.pallas_call(
        pack_kernel,
        out_shape=jax.ShapeDtypeStruct((2,) + keys.shape, keys.dtype),
        in_specs=[ANY, ANY],
        out_specs=VMEM,
        scratch_shapes=[pltpu.SemaphoreType.DMA((2,))],
        compiler_params=pltpu.CompilerParams(vmem_limit_bytes=4 * 1024 * 1024),
        name="pack",
    )(keys, values)


def choose_kernel(index_ref, ends_ref, inner_ref, out_ref):
    place = lax.rem(index_ref[0], 4)
    ends = (place == 0) | (place == 3)

    @pl.when(ends)
    def _():
        out_ref[...] = ends_ref[...]

    @pl.when(jnp.logical_not(ends))
    def _():
        out_ref[...] = inner_ref[...]


def choose(index, ends, inner):
    return pl.pallas_call(
        choose_kernel,
        out_shape=jax.ShapeDtypeStruct(ends.shape, ends.dtype),
        in_specs=[SMEM, VMEM, VMEM],
        out_specs=VMEM,
        compiler_params=pltpu.CompilerParams(vmem_limit_bytes=4 * 1024 * 1024),
        name="choose",
    )(index, ends, inner)


def staged(heads, score, soften, gather):
    for step in range(heads + 2 * LEAD):
        if step < heads:
            score(step)
        if 0 <= step - LEAD < heads:
            soften(step - LEAD)
        if 0 <= step - 2 * LEAD < heads:
            gather(step - 2 * LEAD)


def attend(q_ref, shards, biases, top_ref, total_ref, finish):
    rows, width = q_ref.shape
    scores, state = {}, {}

    def part(which, cols):
        return jnp.concatenate([shard[which, :, cols] for shard in shards], axis=0)

    def score(head):
        cols = head_columns(head)
        scores[head] = lax.dot_general(q_ref[:, cols], part(0, cols), NT, preferred_element_type=jnp.float32)

    def soften(head):
        scaled = scores.pop(head) * SCALE
        parts = [scaled[:, i * rows:(i + 1) * rows] for i in range(len(shards))]
        parts = [p if bias is None else p + bias for p, bias in zip(parts, biases)]
        top = jnp.max(functools.reduce(jnp.maximum, parts), axis=1, keepdims=True)
        kept = None
        if top_ref is not None:
            before = top_ref[head]
            top = jnp.maximum(before, top)
            kept = jnp.exp2(before - top)
        exps = [jnp.exp2(p - top) for p in parts]
        total = jnp.sum(functools.reduce(jnp.add, exps), axis=1, keepdims=True)
        if top_ref is not None:
            total = total_ref[head] * kept + total
        state[head] = (top, kept, total, jnp.concatenate([e.astype(jnp.bfloat16) for e in exps], axis=1))

    def gather(head):
        top, kept, total, weights = state.pop(head)
        summed = jnp.dot(weights, part(1, head_columns(head)), preferred_element_type=jnp.float32)
        finish(head, top, kept, total, summed)

    staged(width // HEAD_DIM, score, soften, gather)


def first_kernel(
    count, index_ref, picks_ref, q_ref, own_ref, mate_ref, one_ref, weight_ref, acc_ref, top_ref,
    total_ref, held_ref, later_ref, sem
):
    fetch = pltpu.make_async_copy(weight_ref, held_ref, sem)
    fetch.start()
    rows = q_ref.shape[0]
    device = index_ref[0]
    biases = [shard_bias(picks_ref, device, by_place(device, offset), count, rows) for offset in FIRST_OFFSETS]
    for i, offset in enumerate(LATER_OFFSETS):
        later_ref[i] = shard_bias(picks_ref, device, by_place(device, offset), count, rows)

    def finish(head, top, kept, total, summed):
        acc_ref[:, head_columns(head)] = summed
        top_ref[head] = jnp.broadcast_to(top, top_ref.shape[1:])
        total_ref[head] = jnp.broadcast_to(total, total_ref.shape[1:])

    attend(q_ref, (own_ref, mate_ref, one_ref), [None, None] + biases, None, None, finish)
    fetch.wait()


def first(count, index, picks, queries, weight, *shards):
    rows, width = queries.shape
    column = jax.ShapeDtypeStruct((width // HEAD_DIM, rows, HEAD_DIM), jnp.float32)
    return pl.pallas_call(
        functools.partial(first_kernel, count),
        out_shape=(jax.ShapeDtypeStruct((rows, width), jnp.float32), column, column,
                   jax.ShapeDtypeStruct(weight.shape, weight.dtype),
                   jax.ShapeDtypeStruct((len(LATER_OFFSETS), rows, rows), jnp.float32)),
        in_specs=[SMEM, SMEM] + [VMEM] * (1 + len(shards)) + [ANY],
        out_specs=(VMEM, VMEM, VMEM, VMEM, VMEM),
        scratch_shapes=[pltpu.SemaphoreType.DMA],
        compiler_params=pltpu.CompilerParams(vmem_limit_bytes=16 * 1024 * 1024),
        name="first",
    )(index, picks, queries, *shards, weight)


def middle_kernel(places, bias_ref, q_ref, acc_ref, top_ref, total_ref, *refs):
    shard_refs = refs[:len(places)]
    new_acc_ref, new_top_ref, new_total_ref = refs[len(places):]

    def finish(head, top, kept, total, summed):
        cols = head_columns(head)
        new_acc_ref[:, cols] = acc_ref[:, cols] * kept + summed
        new_top_ref[head] = top
        new_total_ref[head] = total

    attend(q_ref, shard_refs, [bias_ref[i] for i in places], top_ref, total_ref, finish)


def middle(places, bias, queries, acc, top, total, *shards):
    return pl.pallas_call(
        functools.partial(middle_kernel, places),
        out_shape=[jax.ShapeDtypeStruct(x.shape, x.dtype) for x in (acc, top, total)],
        in_specs=[VMEM] * (5 + len(shards)),
        out_specs=[VMEM, VMEM, VMEM],
        compiler_params=pltpu.CompilerParams(vmem_limit_bytes=16 * 1024 * 1024),
        name="middle",
    )(bias, queries, acc, top, total, *shards)


def last_kernel(
    places, bias_ref, q_ref, acc_ref, top_ref, total_ref, swap_ref, relay_ref, weight_ref, out_ref,
    attended_ref
):
    def finish(head, top, kept, total, summed):
        cols = head_columns(head)
        attended_ref[:, cols] = ((acc_ref[:, cols] * kept + summed) / total).astype(jnp.bfloat16)

    attend(q_ref, (swap_ref, relay_ref), [bias_ref[i] for i in places], top_ref, total_ref, finish)
    out_ref[...] = jnp.dot(attended_ref[...], weight_ref[...], preferred_element_type=jnp.float32).astype(jnp.bfloat16)


def last(places, bias, queries, acc, top, total, *rest):
    rows, width = queries.shape
    return pl.pallas_call(
        functools.partial(last_kernel, places),
        out_shape=jax.ShapeDtypeStruct((rows, width), jnp.bfloat16),
        in_specs=[VMEM] * (5 + len(rest)),
        out_specs=VMEM,
        scratch_shapes=[pltpu.VMEM((rows, width), jnp.bfloat16)],
        compiler_params=pltpu.CompilerParams(vmem_limit_bytes=16 * 1024 * 1024),
        name="last",
    )(bias, queries, acc, top, total, *rest)


def moved(block, steps, origins=(0, 0, 0, 0)):
    count = lax.axis_size("tm")
    route = [(i, i + steps[i % 4]) for i in range(count) if steps[i % 4] and 0 <= i + origins[i % 4] < count]
    return lax.ppermute(block, "tm", [(i, j) for i, j in route if 0 <= j < count])


def body(queries, keys, values, far_picks, out_weight):
    count = lax.axis_size("tm")
    index = lax.axis_index("tm").astype(jnp.int32).reshape(1)
    pair = jnp.stack([keys, values])
    one = moved(pair, STEPS[0])
    two = moved(pair, STEPS[1])
    side = moved(pair, SIDE_STEPS)
    three = moved(choose(index, one, pair), STEPS[2], RELAYED)
    relay = after(moved(one, RELAY_STEPS), 10000000000)
    swap = moved(choose(index, three, one), SWAP_STEPS)
    mate = moved(pair, SWAP_STEPS)
    *state, held, bias = first(count, index, far_picks, queries, out_weight, pair, mate, one)
    state = middle((0, 1), bias, queries, *state, after(two, 30000000000), side)
    state = middle((2,), bias, queries, *state, three)
    return last((3, 4), bias, queries, *state, swap, relay, held)


def solution(mesh):
    placed = (
        P(("vid", "tm"), None),
        P(("vid", "tm"), None),
        P(("vid", "tm"), None),
        P(("vid", "tm"), None),
        P(),
    )
    return jax.shard_map(
        body, mesh=mesh, in_specs=placed, out_specs=P(("vid", "tm"), None), check_vma=False
    )
```

```python
import functools
import math

import jax
import jax.numpy as jnp
from jax import lax
from jax.experimental import pallas as pl
from jax.experimental.pallas import tpu as pltpu
from jax.sharding import PartitionSpec as P

HEAD_DIM = 128
BLK = 64
LEVELS = 2
PICKS = 2
FAR = 8
SCALE = HEAD_DIM ** (-0.5) * math.log2(math.e)
UNUSED = -1e30
LEAD = 4
PIECES = 2
NONE = 1 << 20

STEPS = ((-4, 1, -1, 4), (4, 4, -4, -4), (3, -4, 4, -3))
RELAYED = (4, 0, 0, -4)
SIDE_STEPS = (2, 0, 0, -2)
RELAY_STEPS = (0, 3, -3, 0)
SWAP_STEPS = (1, -1, 1, -1)
FIRST_OFFSETS = ((4, 1, -1, -4),)
LATER_OFFSETS = (
    (-4, -4, 4, 4), (NONE, 2, -2, NONE),
    (-1, 4, -4, 1),
    (2, -2, 2, -2), (-2, NONE, NONE, 2),
)

VMEM = pl.BlockSpec(memory_space=pltpu.VMEM)
SMEM = pl.BlockSpec(memory_space=pltpu.SMEM)
ANY = pl.BlockSpec(memory_space=pl.ANY)
NT = (((1,), (1,)), ((), ()))


def after_kernel(block_ref, out_ref):
    out_ref[...] = block_ref[...]


def after(block, flops):
    return pl.pallas_call(
        after_kernel,
        out_shape=jax.ShapeDtypeStruct(block.shape, block.dtype),
        in_specs=[VMEM],
        out_specs=VMEM,
        cost_estimate=pl.CostEstimate(flops=flops, bytes_accessed=0, transcendentals=0),
        compiler_params=pltpu.CompilerParams(vmem_limit_bytes=4 * 1024 * 1024),
        name="after",
    )(block)


def column_offset(column):
    magnitude = 2 ** (1 + column // PICKS % LEVELS)
    return -magnitude if column < FAR // 2 else magnitude


def head_columns(head):
    return pl.ds(head * HEAD_DIM, HEAD_DIM)


def by_place(device, choices):
    place = lax.rem(device, 4)
    value = jnp.int32(choices[0])
    for i in range(1, 4):
        value = jnp.where(place == i, jnp.int32(choices[i]), value)
    return value


def shard_bias(picks_ref, device, offset, count, rows):
    usable = (device + offset >= 0) & (device + offset < count)
    near = (offset >= -1) & (offset <= 1)
    lane = lax.broadcasted_iota(jnp.int32, (BLK, rows), 1)
    parts = []
    for block in range(rows // BLK):
        bias = jnp.full((BLK, rows), UNUSED, jnp.float32)
        for local in range(rows // BLK):
            named = jnp.where(near, 1, 0)
            for column in range(FAR):
                hit = (picks_ref[block, column] == local) & (offset == column_offset(column))
                named = named + jnp.where(hit, 1, 0)
            named = jnp.where(usable, named, 0)
            value = jnp.where(named == 0, jnp.float32(UNUSED), (named - 1).astype(jnp.float32))
            bias = jnp.where(lane // BLK == local, value, bias)
        parts.append(bias)
    return jnp.concatenate(parts, axis=0)


def pack_kernel(keys_ref, values_ref, pair_ref, sems):
    first = pltpu.make_async_copy(keys_ref, pair_ref.at[0], sems.at[0])
    second = pltpu.make_async_copy(values_ref, pair_ref.at[1], sems.at[1])
    first.start()
    second.start()
    first.wait()
    second.wait()


def pack(keys, values):
    return pl.pallas_call(
        pack_kernel,
        out_shape=jax.ShapeDtypeStruct((2,) + keys.shape, keys.dtype),
        in_specs=[ANY, ANY],
        out_specs=VMEM,
        scratch_shapes=[pltpu.SemaphoreType.DMA((2,))],
        compiler_params=pltpu.CompilerParams(vmem_limit_bytes=4 * 1024 * 1024),
        name="pack",
    )(keys, values)


def choose_kernel(index_ref, ends_ref, inner_ref, out_ref):
    place = lax.rem(index_ref[0], 4)
    ends = (place == 0) | (place == 3)

    @pl.when(ends)
    def _():
        out_ref[...] = ends_ref[...]

    @pl.when(jnp.logical_not(ends))
    def _():
        out_ref[...] = inner_ref[...]


def choose(index, ends, inner):
    return pl.pallas_call(
        choose_kernel,
        out_shape=jax.ShapeDtypeStruct(ends.shape, ends.dtype),
        in_specs=[SMEM, VMEM, VMEM],
        out_specs=VMEM,
        compiler_params=pltpu.CompilerParams(vmem_limit_bytes=4 * 1024 * 1024),
        name="choose",
    )(index, ends, inner)


def staged(heads, score, soften, gather):
    for step in range(heads + 2 * LEAD):
        if step < heads:
            score(step)
        if 0 <= step - LEAD < heads:
            soften(step - LEAD)
        if 0 <= step - 2 * LEAD < heads:
            gather(step - 2 * LEAD)


def attend(q_ref, shards, biases, top_ref, total_ref, finish):
    rows, width = q_ref.shape
    scores, state = {}, {}

    def part(which, cols):
        return jnp.concatenate([shard[which, :, cols] for shard in shards], axis=0)

    def score(head):
        cols = head_columns(head)
        scores[head] = lax.dot_general(q_ref[:, cols], part(0, cols), NT, preferred_element_type=jnp.float32)

    def soften(head):
        scaled = scores.pop(head) * SCALE
        parts = [scaled[:, i * rows:(i + 1) * rows] for i in range(len(shards))]
        parts = [p if bias is None else p + bias for p, bias in zip(parts, biases)]
        top = jnp.max(functools.reduce(jnp.maximum, parts), axis=1, keepdims=True)
        kept = None
        if top_ref is not None:
            before = top_ref[head]
            top = jnp.maximum(before, top)
            kept = jnp.exp2(before - top)
        exps = [jnp.exp2(p - top) for p in parts]
        total = jnp.sum(functools.reduce(jnp.add, exps), axis=1, keepdims=True)
        if top_ref is not None:
            total = total_ref[head] * kept + total
        state[head] = (top, kept, total, jnp.concatenate([e.astype(jnp.bfloat16) for e in exps], axis=1))

    def gather(head):
        top, kept, total, weights = state.pop(head)
        summed = jnp.dot(weights, part(1, head_columns(head)), preferred_element_type=jnp.float32)
        finish(head, top, kept, total, summed)

    staged(width // HEAD_DIM, score, soften, gather)


def first_kernel(
    count, index_ref, picks_ref, q_ref, own_ref, mate_ref, one_ref, weight_ref, acc_ref, top_ref,
    total_ref, held_ref, later_ref, sem
):
    fetch = pltpu.make_async_copy(weight_ref, held_ref, sem)
    fetch.start()
    rows = q_ref.shape[0]
    device = index_ref[0]
    biases = [shard_bias(picks_ref, device, by_place(device, offset), count, rows) for offset in FIRST_OFFSETS]
    for i, offset in enumerate(LATER_OFFSETS):
        later_ref[i] = shard_bias(picks_ref, device, by_place(device, offset), count, rows)

    def finish(head, top, kept, total, summed):
        acc_ref[:, head_columns(head)] = summed
        top_ref[head] = jnp.broadcast_to(top, top_ref.shape[1:])
        total_ref[head] = jnp.broadcast_to(total, total_ref.shape[1:])

    attend(q_ref, (own_ref, mate_ref, one_ref), [None, None] + biases, None, None, finish)
    fetch.wait()


def first(count, index, picks, queries, weight, *shards):
    rows, width = queries.shape
    column = jax.ShapeDtypeStruct((width // HEAD_DIM, rows, HEAD_DIM), jnp.float32)
    return pl.pallas_call(
        functools.partial(first_kernel, count),
        out_shape=(jax.ShapeDtypeStruct((rows, width), jnp.float32), column, column,
                   jax.ShapeDtypeStruct(weight.shape, weight.dtype),
                   jax.ShapeDtypeStruct((len(LATER_OFFSETS), rows, rows), jnp.float32)),
        in_specs=[SMEM, SMEM] + [VMEM] * (1 + len(shards)) + [ANY],
        out_specs=(VMEM, VMEM, VMEM, VMEM, VMEM),
        scratch_shapes=[pltpu.SemaphoreType.DMA],
        compiler_params=pltpu.CompilerParams(vmem_limit_bytes=16 * 1024 * 1024),
        name="first",
    )(index, picks, queries, *shards, weight)


def middle_kernel(places, bias_ref, q_ref, acc_ref, top_ref, total_ref, *refs):
    shard_refs = refs[:len(places)]
    new_acc_ref, new_top_ref, new_total_ref = refs[len(places):]

    def finish(head, top, kept, total, summed):
        cols = head_columns(head)
        new_acc_ref[:, cols] = acc_ref[:, cols] * kept + summed
        new_top_ref[head] = top
        new_total_ref[head] = total

    attend(q_ref, shard_refs, [bias_ref[i] for i in places], top_ref, total_ref, finish)


def middle(places, bias, queries, acc, top, total, *shards):
    return pl.pallas_call(
        functools.partial(middle_kernel, places),
        out_shape=[jax.ShapeDtypeStruct(x.shape, x.dtype) for x in (acc, top, total)],
        in_specs=[VMEM] * (5 + len(shards)),
        out_specs=[VMEM, VMEM, VMEM],
        compiler_params=pltpu.CompilerParams(vmem_limit_bytes=16 * 1024 * 1024),
        name="middle",
    )(bias, queries, acc, top, total, *shards)


def last_kernel(
    places, bias_ref, q_ref, acc_ref, top_ref, total_ref, swap_ref, relay_ref, weight_ref, out_ref,
    attended_ref, mixed_ref, sems
):
    def finish(head, top, kept, total, summed):
        cols = head_columns(head)
        attended_ref[:, cols] = ((acc_ref[:, cols] * kept + summed) / total).astype(jnp.bfloat16)

    attend(q_ref, (swap_ref, relay_ref), [bias_ref[i] for i in places], top_ref, total_ref, finish)
    piece = q_ref.shape[1] // PIECES
    copies = []
    for i in range(PIECES):
        cols = pl.ds(i * piece, piece)
        part = jnp.dot(attended_ref[...], weight_ref[:, cols], preferred_element_type=jnp.float32)
        mixed_ref[:, cols] = part.astype(jnp.bfloat16)
        copies.append(pltpu.make_async_copy(mixed_ref.at[:, cols], out_ref.at[:, cols], sems.at[i]))
        copies[-1].start()
    for copy in copies:
        copy.wait()


def last(places, bias, queries, acc, top, total, *rest):
    rows, width = queries.shape
    return pl.pallas_call(
        functools.partial(last_kernel, places),
        out_shape=jax.ShapeDtypeStruct((rows, width), jnp.bfloat16),
        in_specs=[VMEM] * (5 + len(rest)),
        out_specs=ANY,
        scratch_shapes=[
            pltpu.VMEM((rows, width), jnp.bfloat16),
            pltpu.VMEM((rows, width), jnp.bfloat16),
            pltpu.SemaphoreType.DMA((PIECES,)),
        ],
        compiler_params=pltpu.CompilerParams(vmem_limit_bytes=16 * 1024 * 1024),
        name="last",
    )(bias, queries, acc, top, total, *rest)


def moved(block, steps, origins=(0, 0, 0, 0)):
    count = lax.axis_size("tm")
    route = [(i, i + steps[i % 4]) for i in range(count) if steps[i % 4] and 0 <= i + origins[i % 4] < count]
    return lax.ppermute(block, "tm", [(i, j) for i, j in route if 0 <= j < count])


def body(queries, keys, values, far_picks, out_weight):
    count = lax.axis_size("tm")
    index = lax.axis_index("tm").astype(jnp.int32).reshape(1)
    pair = jnp.stack([keys, values])
    one = moved(pair, STEPS[0])
    two = moved(pair, STEPS[1])
    side = moved(pair, SIDE_STEPS)
    three = moved(choose(index, one, pair), STEPS[2], RELAYED)
    relay = after(moved(one, RELAY_STEPS), 10000000000)
    swap = moved(choose(index, three, one), SWAP_STEPS)
    mate = moved(pair, SWAP_STEPS)
    *state, held, bias = first(count, index, far_picks, queries, out_weight, pair, mate, one)
    state = middle((0,), bias, queries, *state, after(two, 30000000000))
    state = middle((1, 2), bias, queries, *state, side, three)
    return last((3, 4), bias, queries, *state, swap, relay, held)


def solution(mesh):
    placed = (
        P(("vid", "tm"), None),
        P(("vid", "tm"), None),
        P(("vid", "tm"), None),
        P(("vid", "tm"), None),
        P(),
    )
    return jax.shard_map(
        body, mesh=mesh, in_specs=placed, out_specs=P(("vid", "tm"), None), check_vma=False
    )
```

```python
import functools
import math

import jax
import jax.numpy as jnp
from jax import lax
from jax.experimental import pallas as pl
from jax.experimental.pallas import tpu as pltpu
from jax.sharding import PartitionSpec as P

HEAD_DIM = 128
BLK = 64
LEVELS = 2
PICKS = 2
FAR = 8
SCALE = HEAD_DIM ** (-0.5) * math.log2(math.e)
UNUSED = -1e30
LEAD = 6
PIECES = 2
NONE = 1 << 20

STEPS = ((-4, 1, -1, 4), (4, 4, -4, -4), (3, -4, 4, -3))
RELAYED = (4, 0, 0, -4)
SIDE_STEPS = (2, 0, 0, -2)
RELAY_STEPS = (0, 3, -3, 0)
SWAP_STEPS = (1, -1, 1, -1)
FIRST_OFFSETS = ((4, 1, -1, -4),)
LATER_OFFSETS = (
    (-4, -4, 4, 4), (NONE, 2, -2, NONE),
    (-1, 4, -4, 1),
    (2, -2, 2, -2), (-2, NONE, NONE, 2),
)

VMEM = pl.BlockSpec(memory_space=pltpu.VMEM)
SMEM = pl.BlockSpec(memory_space=pltpu.SMEM)
ANY = pl.BlockSpec(memory_space=pl.ANY)
NT = (((1,), (1,)), ((), ()))


def after_kernel(block_ref, out_ref):
    out_ref[...] = block_ref[...]


def after(block, flops):
    return pl.pallas_call(
        after_kernel,
        out_shape=jax.ShapeDtypeStruct(block.shape, block.dtype),
        in_specs=[VMEM],
        out_specs=VMEM,
        cost_estimate=pl.CostEstimate(flops=flops, bytes_accessed=0, transcendentals=0),
        compiler_params=pltpu.CompilerParams(vmem_limit_bytes=4 * 1024 * 1024),
        name="after",
    )(block)


def column_offset(column):
    magnitude = 2 ** (1 + column // PICKS % LEVELS)
    return -magnitude if column < FAR // 2 else magnitude


def head_columns(head):
    return pl.ds(head * HEAD_DIM, HEAD_DIM)


def by_place(device, choices):
    place = lax.rem(device, 4)
    value = jnp.int32(choices[0])
    for i in range(1, 4):
        value = jnp.where(place == i, jnp.int32(choices[i]), value)
    return value


def shard_bias(picks_ref, device, offset, count, rows):
    usable = (device + offset >= 0) & (device + offset < count)
    near = (offset >= -1) & (offset <= 1)
    lane = lax.broadcasted_iota(jnp.int32, (BLK, rows), 1)
    parts = []
    for block in range(rows // BLK):
        bias = jnp.full((BLK, rows), UNUSED, jnp.float32)
        for local in range(rows // BLK):
            named = jnp.where(near, 1, 0)
            for column in range(FAR):
                hit = (picks_ref[block, column] == local) & (offset == column_offset(column))
                named = named + jnp.where(hit, 1, 0)
            named = jnp.where(usable, named, 0)
            value = jnp.where(named == 0, jnp.float32(UNUSED), (named - 1).astype(jnp.float32))
            bias = jnp.where(lane // BLK == local, value, bias)
        parts.append(bias)
    return jnp.concatenate(parts, axis=0)


def pack_kernel(keys_ref, values_ref, pair_ref, sems):
    first = pltpu.make_async_copy(keys_ref, pair_ref.at[0], sems.at[0])
    second = pltpu.make_async_copy(values_ref, pair_ref.at[1], sems.at[1])
    first.start()
    second.start()
    first.wait()
    second.wait()


def pack(keys, values):
    return pl.pallas_call(
        pack_kernel,
        out_shape=jax.ShapeDtypeStruct((2,) + keys.shape, keys.dtype),
        in_specs=[ANY, ANY],
        out_specs=VMEM,
        scratch_shapes=[pltpu.SemaphoreType.DMA((2,))],
        compiler_params=pltpu.CompilerParams(vmem_limit_bytes=4 * 1024 * 1024),
        name="pack",
    )(keys, values)


def choose_kernel(index_ref, ends_ref, inner_ref, out_ref):
    place = lax.rem(index_ref[0], 4)
    ends = (place == 0) | (place == 3)

    @pl.when(ends)
    def _():
        out_ref[...] = ends_ref[...]

    @pl.when(jnp.logical_not(ends))
    def _():
        out_ref[...] = inner_ref[...]


def choose(index, ends, inner):
    return pl.pallas_call(
        choose_kernel,
        out_shape=jax.ShapeDtypeStruct(ends.shape, ends.dtype),
        in_specs=[SMEM, VMEM, VMEM],
        out_specs=VMEM,
        compiler_params=pltpu.CompilerParams(vmem_limit_bytes=4 * 1024 * 1024),
        name="choose",
    )(index, ends, inner)


def staged(heads, score, soften, gather):
    for step in range(heads + 2 * LEAD):
        if step < heads:
            score(step)
        if 0 <= step - LEAD < heads:
            soften(step - LEAD)
        if 0 <= step - 2 * LEAD < heads:
            gather(step - 2 * LEAD)


def attend(q_ref, shards, biases, top_ref, total_ref, finish):
    rows, width = q_ref.shape
    scores, state = {}, {}

    def part(which, cols):
        return jnp.concatenate([shard[which, :, cols] for shard in shards], axis=0)

    def score(head):
        cols = head_columns(head)
        scores[head] = lax.dot_general(q_ref[:, cols], part(0, cols), NT, preferred_element_type=jnp.float32)

    def soften(head):
        scaled = scores.pop(head) * SCALE
        parts = [scaled[:, i * rows:(i + 1) * rows] for i in range(len(shards))]
        parts = [p if bias is None else p + bias for p, bias in zip(parts, biases)]
        top = jnp.max(functools.reduce(jnp.maximum, parts), axis=1, keepdims=True)
        kept = None
        if top_ref is not None:
            before = top_ref[head]
            top = jnp.maximum(before, top)
            kept = jnp.exp2(before - top)
        exps = [jnp.exp2(p - top) for p in parts]
        total = jnp.sum(functools.reduce(jnp.add, exps), axis=1, keepdims=True)
        if top_ref is not None:
            total = total_ref[head] * kept + total
        state[head] = (top, kept, total, jnp.concatenate([e.astype(jnp.bfloat16) for e in exps], axis=1))

    def gather(head):
        top, kept, total, weights = state.pop(head)
        summed = jnp.dot(weights, part(1, head_columns(head)), preferred_element_type=jnp.float32)
        finish(head, top, kept, total, summed)

    staged(width // HEAD_DIM, score, soften, gather)


def first_kernel(
    count, index_ref, picks_ref, q_ref, own_ref, mate_ref, one_ref, weight_ref, acc_ref, top_ref,
    total_ref, held_ref, later_ref, sem
):
    fetch = pltpu.make_async_copy(weight_ref, held_ref, sem)
    fetch.start()
    rows = q_ref.shape[0]
    device = index_ref[0]
    biases = [shard_bias(picks_ref, device, by_place(device, offset), count, rows) for offset in FIRST_OFFSETS]
    for i, offset in enumerate(LATER_OFFSETS):
        later_ref[i] = shard_bias(picks_ref, device, by_place(device, offset), count, rows)

    def finish(head, top, kept, total, summed):
        acc_ref[:, head_columns(head)] = summed
        top_ref[head] = jnp.broadcast_to(top, top_ref.shape[1:])
        total_ref[head] = jnp.broadcast_to(total, total_ref.shape[1:])

    attend(q_ref, (own_ref, mate_ref, one_ref), [None, None] + biases, None, None, finish)
    fetch.wait()


def first(count, index, picks, queries, weight, *shards):
    rows, width = queries.shape
    column = jax.ShapeDtypeStruct((width // HEAD_DIM, rows, HEAD_DIM), jnp.float32)
    return pl.pallas_call(
        functools.partial(first_kernel, count),
        out_shape=(jax.ShapeDtypeStruct((rows, width), jnp.float32), column, column,
                   jax.ShapeDtypeStruct(weight.shape, weight.dtype),
                   jax.ShapeDtypeStruct((len(LATER_OFFSETS), rows, rows), jnp.float32)),
        in_specs=[SMEM, SMEM] + [VMEM] * (1 + len(shards)) + [ANY],
        out_specs=(VMEM, VMEM, VMEM, VMEM, VMEM),
        scratch_shapes=[pltpu.SemaphoreType.DMA],
        compiler_params=pltpu.CompilerParams(vmem_limit_bytes=16 * 1024 * 1024),
        name="first",
    )(index, picks, queries, *shards, weight)


def middle_kernel(places, bias_ref, q_ref, acc_ref, top_ref, total_ref, *refs):
    shard_refs = refs[:len(places)]
    new_acc_ref, new_top_ref, new_total_ref = refs[len(places):]

    def finish(head, top, kept, total, summed):
        cols = head_columns(head)
        new_acc_ref[:, cols] = acc_ref[:, cols] * kept + summed
        new_top_ref[head] = top
        new_total_ref[head] = total

    attend(q_ref, shard_refs, [bias_ref[i] for i in places], top_ref, total_ref, finish)


def middle(places, bias, queries, acc, top, total, *shards):
    return pl.pallas_call(
        functools.partial(middle_kernel, places),
        out_shape=[jax.ShapeDtypeStruct(x.shape, x.dtype) for x in (acc, top, total)],
        in_specs=[VMEM] * (5 + len(shards)),
        out_specs=[VMEM, VMEM, VMEM],
        compiler_params=pltpu.CompilerParams(vmem_limit_bytes=16 * 1024 * 1024),
        name="middle",
    )(bias, queries, acc, top, total, *shards)


def last_kernel(
    places, bias_ref, q_ref, acc_ref, top_ref, total_ref, swap_ref, relay_ref, weight_ref, out_ref,
    attended_ref, mixed_ref, sems
):
    def finish(head, top, kept, total, summed):
        cols = head_columns(head)
        attended_ref[:, cols] = ((acc_ref[:, cols] * kept + summed) / total).astype(jnp.bfloat16)

    attend(q_ref, (swap_ref, relay_ref), [bias_ref[i] for i in places], top_ref, total_ref, finish)
    piece = q_ref.shape[1] // PIECES
    copies = []
    for i in range(PIECES):
        cols = pl.ds(i * piece, piece)
        part = jnp.dot(attended_ref[...], weight_ref[:, cols], preferred_element_type=jnp.float32)
        mixed_ref[:, cols] = part.astype(jnp.bfloat16)
        copies.append(pltpu.make_async_copy(mixed_ref.at[:, cols], out_ref.at[:, cols], sems.at[i]))
        copies[-1].start()
    for copy in copies:
        copy.wait()


def last(places, bias, queries, acc, top, total, *rest):
    rows, width = queries.shape
    return pl.pallas_call(
        functools.partial(last_kernel, places),
        out_shape=jax.ShapeDtypeStruct((rows, width), jnp.bfloat16),
        in_specs=[VMEM] * (5 + len(rest)),
        out_specs=ANY,
        scratch_shapes=[
            pltpu.VMEM((rows, width), jnp.bfloat16),
            pltpu.VMEM((rows, width), jnp.bfloat16),
            pltpu.SemaphoreType.DMA((PIECES,)),
        ],
        compiler_params=pltpu.CompilerParams(vmem_limit_bytes=16 * 1024 * 1024),
        name="last",
    )(bias, queries, acc, top, total, *rest)


def moved(block, steps, origins=(0, 0, 0, 0)):
    count = lax.axis_size("tm")
    route = [(i, i + steps[i % 4]) for i in range(count) if steps[i % 4] and 0 <= i + origins[i % 4] < count]
    return lax.ppermute(block, "tm", [(i, j) for i, j in route if 0 <= j < count])


def body(queries, keys, values, far_picks, out_weight):
    count = lax.axis_size("tm")
    index = lax.axis_index("tm").astype(jnp.int32).reshape(1)
    pair = jnp.stack([keys, values])
    one = moved(pair, STEPS[0])
    two = moved(pair, STEPS[1])
    side = moved(pair, SIDE_STEPS)
    three = moved(choose(index, one, pair), STEPS[2], RELAYED)
    relay = after(moved(one, RELAY_STEPS), 10000000000)
    swap = moved(choose(index, three, one), SWAP_STEPS)
    mate = moved(pair, SWAP_STEPS)
    *state, held, bias = first(count, index, far_picks, queries, out_weight, pair, mate, one)
    state = middle((0,), bias, queries, *state, after(two, 30000000000))
    state = middle((1, 2), bias, queries, *state, side, three)
    return last((3, 4), bias, queries, *state, swap, relay, held)


def solution(mesh):
    placed = (
        P(("vid", "tm"), None),
        P(("vid", "tm"), None),
        P(("vid", "tm"), None),
        P(("vid", "tm"), None),
        P(),
    )
    return jax.shard_map(
        body, mesh=mesh, in_specs=placed, out_specs=P(("vid", "tm"), None), check_vma=False
    )
```
